32 devices in a mesh: member: 2 (over y), wave: 4 (over z), level: 2 (over x), fld: 2 (over core).
Axes of the slice: x: 2, y: 2, z: 4, core: 2. Of those that a mesh axis runs over, the one named last changes fastest.
Arguments:
- grid_state: bfloat16 [256, 2, 256, 1536], P(('member', 'level'), 'fld', 'wave'), parts along dimension 0, may hold values from -6 to 6
- legendre: bfloat16 [512, 2, 256, 256], P(('wave', 'level'), 'fld'), may hold values from -0.375 to 0.375
- wave_order: int32 [512], replicated, may hold values from 0 to 511, each once
- lat_order: int32 [256], replicated, may hold values from 0 to 255, each once
- eig_rates: float32 [128], replicated, may hold values from 0.1 to 4
- modes_in: bfloat16 [128, 128], replicated, may hold values from -0.5 to 0.5
- modes_out: bfloat16 [128, 128], replicated, may hold values from -0.5 to 0.5
Outputs:
- new_state: bfloat16 [256, 2, 256, 1536], P(('member', 'level'), 'fld', 'wave'), parts along dimension 0
The draws below stay inside these ranges and needn't reach their ends.
There are 2 independent parts, one for each index of `member`. The reference program is written for one: setup_inputs(seed, part) draws one part's arguments, and reference() takes and returns one part's arrays. A program takes and returns all parts, laid end to end along the dimension named above; an argument that names none is the same for every part. Nothing has to cross between parts.
Inputs may be any that keep to these rules, and one draw needn't show every extreme that they name: Slot s holds zonal wavenumber wave_order[s]; every wavenumber 0 to 511 is held by exactly one slot. Latitude row r lies at Gaussian latitude index lat_order[r] counted from the equator, the same in both hemispheres; every index appears once.
All inputs are finite; a program needn't handle non-finite values.
Results may differ from the reference program's by a relative error of at most 0.0098.
Values may be sent and summed in bfloat16 or wider, within the bound.
A program may use at most 128 MiB of HBM per device.

```python
import math
import jax
import jax.numpy as jnp
from jax import lax

LON = 1536
LATH = 256
M = 512
NH = 256
LEV = 128
ITERS = 1


def level_of(rng, extent, split, least, high):
    loudness = 1.0
    for dim, parts in split:
        steps = jax.random.uniform(jax.random.fold_in(jax.random.fold_in(rng, 6), dim), (parts,), jnp.float32, least / len(split), high / len(split))
        loudness = loudness * jnp.repeat(jnp.exp(steps), extent[dim] // parts).reshape((-1,) + (1,) * (len(extent) - 1 - dim))
    return loudness


def scatter_about(stream_key, extent, deviation, bound, cuts=(), kind=jnp.bfloat16):
    entries = jax.random.normal(stream_key, extent, jnp.float32) * deviation
    if len(cuts) > 0:
        entries = level_of(stream_key, extent, cuts, -0.22, 0.18) * entries
    return jnp.clip(entries, min=-bound, max=bound).astype(kind)


def setup_inputs(seed: int = 0, part: int = 0) -> dict:
    key_list = jax.random.split(jax.random.key(seed), 8)
    own_keys = jax.random.split(jax.random.fold_in(key_list[7], part), 8)
    grid_state = scatter_about(own_keys[0], (LEV, 2, LATH, LON), 1.0, 6.0, ((0, 2), (1, 2), (2, 4)))
    legendre = scatter_about(key_list[1], (M, 2, LATH, NH), NH ** -0.5, 0.375, ((0, 8), (1, 2)))
    wave_order = jax.random.permutation(key_list[2], M).astype(jnp.int32)
    lat_order = jax.random.permutation(key_list[3], LATH).astype(jnp.int32)
    eig_rates = jnp.clip(jnp.exp(jax.random.uniform(key_list[4], (LEV,), jnp.float32, math.log(0.1), math.log(4.0))), 0.1, 4.0)
    modes_in = scatter_about(key_list[5], (LEV, LEV), LEV ** -0.5, 0.5)
    modes_out = scatter_about(key_list[6], (LEV, LEV), LEV ** -0.5, 0.5)
    return dict(grid_state=grid_state, legendre=legendre, wave_order=wave_order, lat_order=lat_order, eig_rates=eig_rates, modes_in=modes_in, modes_out=modes_out)


tau_scale = 2.0

def fourier_table(wave_order, lon_count):
    longitude = jnp.arange(lon_count, dtype=jnp.int32)
    phase_index = longitude[:, None] * wave_order[None, :].astype(jnp.int32) % lon_count
    angles = phase_index.astype(jnp.float32) * (2.0 * math.pi / lon_count)
    weight_scale = math.sqrt(2.0 / lon_count)
    return jnp.concatenate([jnp.cos(angles) * weight_scale, -jnp.sin(angles) * weight_scale], axis=1).astype(jnp.bfloat16)

def rounded(values):
    return lax.optimization_barrier(values.astype(jnp.bfloat16)).astype(jnp.float32)

def reference(grid_state, legendre, wave_order, lat_order, eig_rates, modes_in, modes_out):
    highest = lax.Precision.HIGHEST
    wave_table = fourier_table(wave_order, LON).astype(jnp.float32)
    sine = jnp.sin((lat_order.astype(jnp.float32) + 0.5) * (math.pi / (2.0 * LATH)))
    hemi_sign = jnp.array([1.0, -1.0], dtype=jnp.float32)
    coupling = (0.5 * hemi_sign)[None, :, None, None] * sine[None, None, :, None]
    parity = jnp.arange(2, dtype=jnp.int32)
    degree = wave_order.astype(jnp.int32)[:, None, None] + 2 * jnp.arange(NH, dtype=jnp.int32)[None, None, :] + parity[None, :, None]
    in_triangle = (degree <= M - 1).astype(jnp.float32)
    degree_f = degree.astype(jnp.float32)
    damp_ratio = tau_scale * degree_f * (degree_f + 1.0) / float(M * (M - 1))
    factor = 1.0 / (1.0 + damp_ratio[..., None] * eig_rates[None, None, None, :])
    table_f = legendre.astype(jnp.float32)
    inward = modes_in.astype(jnp.float32)
    outward = modes_out.astype(jnp.float32)
    initial = grid_state.astype(jnp.float32)
    current = grid_state
    for iteration in range(ITERS):
        forcing = (initial + coupling * jnp.tanh(current.astype(jnp.float32))).astype(jnp.bfloat16)
        fourier_rows = jnp.einsum('lhrg,gk->lhrk', forcing.astype(jnp.float32), wave_table, precision=highest)
        fourier_rows = rounded(fourier_rows).reshape(LEV, 2, LATH, 2, M)
        mirrored = jnp.stack([fourier_rows[:, 0] + fourier_rows[:, 1], fourier_rows[:, 0] - fourier_rows[:, 1]], axis=1)
        mirrored = rounded(mirrored)
        spectral = jnp.einsum('lprcs,sprj->spjcl', mirrored, table_f, precision=highest)
        spectral = rounded(spectral * in_triangle[:, :, :, None, None])
        modal = jnp.einsum('spjcl,kl->spjck', spectral, inward, precision=highest)
        modal = rounded(modal * factor[:, :, :, None, :])
        solved = rounded(jnp.einsum('spjck,lk->spjcl', modal, outward, precision=highest))
        grid_coeffs = rounded(jnp.einsum('spjcl,sprj->lprcs', solved, table_f, precision=highest))
        hemi_grid = jnp.stack([0.5 * (grid_coeffs[:, 0] + grid_coeffs[:, 1]), 0.5 * (grid_coeffs[:, 0] - grid_coeffs[:, 1])], axis=1)
        flat_coeffs = rounded(hemi_grid).reshape(LEV, 2, LATH, 2 * M)
        current = jnp.einsum('lhrk,gk->lhrg', flat_coeffs, wave_table, precision=highest).astype(jnp.bfloat16)
    return current
```

```python
import functools
import math

import jax
import jax.numpy as jnp
import numpy as np
from jax import lax
from jax.experimental import pallas as pl
from jax.experimental.pallas import tpu as pltpu
from jax.sharding import PartitionSpec as P

LANES = 128
PACK = 16
SLOT_CHUNKS = 1
SLOTS_PER_STEP = 4
VMEM = 60 * 1024 * 1024

tau_scale = 2.0


def partner(value, axis, stride):
    mask = 2**stride
    pairs = [(source, source ^ mask) for source in range(lax.axis_size(axis))]
    return lax.ppermute(value, axis, pairs)


def fourier_table(wave_order, lon_count):
    longitude = jnp.arange(lon_count, dtype=jnp.int32)
    phase_index = longitude[:, None] * wave_order[None, :] % lon_count
    angles = phase_index.astype(jnp.float32) * (2.0 * math.pi / lon_count)
    weight_scale = math.sqrt(2.0 / lon_count)
    return jnp.concatenate(
        [jnp.cos(angles) * weight_scale, -jnp.sin(angles) * weight_scale], axis=1
    ).astype(jnp.bfloat16)


def degrees(wave_ids, parity, half_count):
    return wave_ids[:, None] + 2 * jnp.arange(half_count, dtype=jnp.int32)[None, :] + parity


def triangle_mask(wave_ids, parity, half_count, wave_count):
    return (degrees(wave_ids, parity, half_count) <= wave_count - 1).astype(jnp.float32)


def damping(wave_ids, parity, half_count, wave_count, eig_rates):
    degree_f = degrees(wave_ids, parity, half_count).astype(jnp.float32)
    damp_ratio = tau_scale * degree_f * (degree_f + 1.0) / float(wave_count * (wave_count - 1))
    return 1.0 / (1.0 + damp_ratio[:, :, None] * eig_rates[None, None, :])


def forward_legendre(mirrored, table_part, in_triangle):
    spectral = jnp.einsum(
        "lhrcs,shrj->sjcl", mirrored, table_part, preferred_element_type=jnp.float32
    )
    return (spectral * in_triangle[:, :, None, None]).astype(jnp.bfloat16)


def inverse_legendre(solved, table_part):
    return jnp.einsum(
        "sjcl,shrj->lhrcs", solved, table_part, preferred_element_type=jnp.float32
    ).astype(jnp.bfloat16)


def implicit_solve(columns, factor, modes_in, modes_out):
    modal = jnp.einsum("sjcl,kl->sjck", columns, modes_in, preferred_element_type=jnp.float32)
    modal = (modal * factor[:, :, None, :]).astype(jnp.bfloat16)
    return jnp.einsum("sjck,lk->sjcl", modal, modes_out, preferred_element_type=jnp.float32).astype(
        jnp.bfloat16
    )


def general_shards(grid_state, legendre, wave_order, lat_order, eig_rates, modes_in, modes_out):
    lon_count = grid_state.shape[3]
    rows_here = grid_state.shape[2]
    wave_count = wave_order.shape[0]
    half_rows = lat_order.shape[0]
    half_count = legendre.shape[3]
    wave_size = lax.axis_size("wave")
    level_size = lax.axis_size("level")
    parity = lax.axis_index("fld")
    wave_place = lax.axis_index("wave")
    level_place = lax.axis_index("level")
    wave_table = fourier_table(wave_order, lon_count)
    lat_rows = lax.dynamic_slice_in_dim(lat_order, wave_place * rows_here, rows_here)
    sine = jnp.sin((lat_rows.astype(jnp.float32) + 0.5) * (math.pi / (2.0 * half_rows)))
    hemi_sign = 1.0 - 2.0 * parity.astype(jnp.float32)
    coupling = (0.5 * hemi_sign * sine)[None, None, :, None]
    wide_count = wave_count // wave_size
    narrow_count = wide_count // level_size
    wide_start = wave_place * wide_count
    narrow_start = wide_start + level_place * narrow_count
    wide_waves = lax.dynamic_slice_in_dim(wave_order, wide_start, wide_count)
    narrow_waves = lax.dynamic_slice_in_dim(wave_order, narrow_start, narrow_count)
    factor = damping(narrow_waves, parity, half_count, wave_count, eig_rates)
    wide_table = lax.all_gather(legendre, "level", axis=0, tiled=True)
    wide_mask = triangle_mask(wide_waves, parity, half_count, wave_count)
    initial = grid_state.astype(jnp.float32)
    current = grid_state
    forcing = (initial + coupling * jnp.tanh(current.astype(jnp.float32))).astype(jnp.bfloat16)
    fourier_rows = jnp.einsum(
        "lhrg,gk->lhrk", forcing, wave_table, preferred_element_type=jnp.float32
    )
    fourier_rows = fourier_rows.astype(jnp.bfloat16).reshape(
        fourier_rows.shape[:3] + (2, wave_count)
    )
    mirror_part = partner(fourier_rows, "fld", 0)
    mirrored = (
        mirror_part.astype(jnp.float32) + hemi_sign * fourier_rows.astype(jnp.float32)
    ).astype(jnp.bfloat16)
    gathered = lax.all_to_all(mirrored, "wave", split_axis=4, concat_axis=2, tiled=True)
    spectral = forward_legendre(gathered, wide_table, wide_mask)
    columns = lax.all_to_all(spectral, "level", split_axis=0, concat_axis=3, tiled=True)
    solved = implicit_solve(columns, factor, modes_in, modes_out)
    level_rows = lax.all_to_all(solved, "level", split_axis=3, concat_axis=0, tiled=True)
    grid_coeffs = inverse_legendre(level_rows, wide_table)
    grid_coeffs = lax.all_to_all(grid_coeffs, "wave", split_axis=2, concat_axis=4, tiled=True)
    mirror_back = partner(grid_coeffs, "fld", 0)
    hemi_grid = (
        0.5 * (mirror_back.astype(jnp.float32) + hemi_sign * grid_coeffs.astype(jnp.float32))
    ).astype(jnp.bfloat16)
    flat_coeffs = hemi_grid.reshape(hemi_grid.shape[:3] + (2 * wave_count,))
    current = jnp.einsum(
        "lhrk,gk->lhrg", flat_coeffs, wave_table, preferred_element_type=jnp.float32
    ).astype(jnp.bfloat16)
    return current


def selected_table(wave_order, lon_count):
    wave_count = wave_order.shape[0]
    phase = np.arange(wave_count)[:, None] * np.arange(lon_count)[None, :] % lon_count
    angles = phase * (2.0 * math.pi / lon_count)
    rows = np.stack([np.cos(angles), -np.sin(angles)], axis=1) * math.sqrt(2.0 / lon_count)
    rows = jnp.asarray(rows.reshape(2 * wave_count, lon_count).astype(np.float32), jnp.bfloat16)
    wanted = 2 * wave_order[:, None] + jnp.arange(2, dtype=jnp.int32)[None, :]
    held = jnp.arange(2 * wave_count, dtype=jnp.int32)
    pick = (wanted.reshape(-1, 1) == held[None, :]).astype(jnp.bfloat16)
    return jnp.dot(pick, rows, preferred_element_type=jnp.float32).astype(jnp.bfloat16)


def forward_kernel(coupling_ref, state_ref, table_ref, out_ref, turned):
    step = pl.program_id(1)
    levels, rows, lon = state_ref.shape
    groups = levels * rows // LANES
    initial = state_ref[...].astype(jnp.float32)
    forcing = (initial + coupling_ref[...] * jnp.tanh(initial)).astype(jnp.bfloat16)
    forcing = forcing.reshape(levels * rows, lon)
    coeffs = lax.dot_general(
        table_ref[...], forcing, (((1,), (1,)), ((), ())), preferred_element_type=jnp.float32
    )
    for group in range(groups):
        turned[pl.ds(step * groups + group, coeffs.shape[0], stride=PACK), :] = coeffs[
            :, group * LANES : (group + 1) * LANES
        ]

    @pl.when(step == pl.num_programs(1) - 1)
    def _():
        out_ref[...] = turned[...].reshape(out_ref.shape).astype(jnp.bfloat16)


def forward_rows(state, table, coupling):
    levels, rows, lon = state.shape
    row_count = table.shape[0]
    halves = levels * rows // (LANES * PACK)
    step_levels = max(1, 256 // rows)
    steps = levels // halves // step_levels
    return pl.pallas_call(
        forward_kernel,
        grid=(halves, steps),
        in_specs=[
            pl.BlockSpec((1, rows, 1), lambda h, t: (0, 0, 0)),
            pl.BlockSpec((step_levels, rows, lon), lambda h, t: (h * steps + t, 0, 0)),
            pl.BlockSpec((row_count, lon), lambda h, t: (0, 0)),
        ],
        out_specs=pl.BlockSpec((row_count, PACK, LANES), lambda h, t: (0, h, 0)),
        out_shape=jax.ShapeDtypeStruct((row_count, halves * PACK, LANES), jnp.bfloat16),
        scratch_shapes=[pltpu.VMEM((row_count * PACK, LANES), jnp.float32)],
        compiler_params=pltpu.CompilerParams(vmem_limit_bytes=VMEM),
        cost_estimate=pl.CostEstimate(
            flops=2 * levels * rows * lon * row_count,
            bytes_accessed=2 * (state.size + table.size + row_count * levels * rows),
            transcendentals=state.size,
        ),
    )(coupling, state, table)


def spectral_kernel(rows, data_ref, table_ref, mask_ref, ratio_ref, eig_ref, in_ref, out_modes, out_ref):
    waves, places, slots, lines, _ = data_ref.shape
    parts = LANES // rows
    modes = eig_ref.shape[0]
    for slot in range(slots):
        picked = []
        for part in range(parts):
            for place in range(places):
                picked.append(
                    jnp.concatenate(
                        [
                            data_ref[wave, place, slot][:, part * rows : (part + 1) * rows]
                            for wave in range(waves)
                        ],
                        axis=1,
                    )
                )
        table = table_ref[slot]
        spectral = jnp.dot(
            jnp.concatenate(picked, axis=0), table, preferred_element_type=jnp.float32
        )
        spectral = (spectral * mask_ref[slot]).astype(jnp.bfloat16)
        modal = jnp.dot(in_ref[...], spectral, preferred_element_type=jnp.float32)
        factor = 1.0 / (1.0 + eig_ref[...] * ratio_ref[slot])
        modal = jnp.concatenate(
            [modal[:modes] * factor, modal[modes:] * factor], axis=0
        ).astype(jnp.bfloat16)
        solved = jnp.dot(out_modes[...], modal, preferred_element_type=jnp.float32)
        coeffs = lax.dot_general(
            solved.astype(jnp.bfloat16),
            table,
            (((1,), (1,)), ((), ())),
            preferred_element_type=jnp.float32,
        ).astype(jnp.bfloat16)
        for wave in range(waves):
            for place in range(places):
                out_ref[wave, place, slot] = jnp.concatenate(
                    [
                        coeffs[
                            (part * places + place) * lines : (part * places + place + 1) * lines,
                            wave * rows : (wave + 1) * rows,
                        ]
                        for part in range(parts)
                    ],
                    axis=1,
                )


def spectral_step(data, legendre, first, mask, ratio, eig_rates, inward, outward, rows):
    waves, places, slots, lines, _ = data.shape
    half_rows, half_count = legendre.shape[1:]
    modes = eig_rates.shape[0]
    block = math.gcd(slots, SLOTS_PER_STEP)
    skip = first // block
    whole = pl.BlockSpec(inward.shape, lambda i: (0, 0))
    vector = pl.BlockSpec((block, 1, half_count), lambda i: (i + skip, 0, 0))
    moved = pl.BlockSpec((waves, places, block, lines, LANES), lambda i: (0, 0, i, 0, 0))
    return pl.pallas_call(
        functools.partial(spectral_kernel, rows),
        grid=(slots // block,),
        in_specs=[
            moved,
            pl.BlockSpec((block, half_rows, half_count), lambda i: (i + skip, 0, 0)),
            vector,
            vector,
            pl.BlockSpec((modes, 1), lambda i: (0, 0)),
            whole,
            whole,
        ],
        out_specs=moved,
        out_shape=jax.ShapeDtypeStruct(data.shape, jnp.bfloat16),
        compiler_params=pltpu.CompilerParams(vmem_limit_bytes=VMEM),
        cost_estimate=pl.CostEstimate(
            flops=8 * slots * half_rows * half_count * inward.shape[0],
            bytes_accessed=2 * (2 * data.size + slots * half_rows * half_count),
            transcendentals=0,
        ),
    )(data, legendre, mask, ratio, eig_rates.reshape(-1, 1), inward, outward)


def inverse_kernel(chunks, sign_ref, *refs):
    own_refs, other_refs = refs[:chunks], refs[chunks : 2 * chunks]
    table_ref, out_ref, turned = refs[2 * chunks :]
    step = pl.program_id(1)
    levels, rows, lon = out_ref.shape
    groups = levels * rows // LANES
    blocks, chunk_rows = own_refs[0].shape[:2]

    @pl.when(step == 0)
    def _():
        for block in range(blocks):
            for chunk in range(chunks):
                own = own_refs[chunk][block].astype(jnp.float32)
                other = other_refs[chunk][block].astype(jnp.float32)
                grid = (0.5 * (other + sign_ref[0] * own)).astype(jnp.bfloat16)
                first = (block * chunks + chunk) * chunk_rows * PACK
                turned[first : first + chunk_rows * PACK, :] = grid.astype(jnp.float32).reshape(
                    -1, LANES
                )

    picked = jnp.concatenate(
        [
            turned[
                pl.ds(step * groups + group, blocks * chunks * chunk_rows, stride=PACK), :
            ].astype(jnp.bfloat16)
            for group in range(groups)
        ],
        axis=1,
    )
    out = lax.dot_general(
        picked, table_ref[...], (((0,), (0,)), ((), ())), preferred_element_type=jnp.float32
    )
    out_ref[...] = out.astype(jnp.bfloat16).reshape(out_ref.shape)


def inverse_rows(own, other, table, sign, levels, rows):
    chunks = len(own)
    blocks, chunk_rows = own[0].shape[:2]
    row_count, lon = table.shape
    halves = levels * rows // (LANES * PACK)
    step_levels = max(1, 256 // rows)
    steps = levels // halves // step_levels
    moved = pl.BlockSpec((blocks, chunk_rows, PACK, LANES), lambda h, t: (0, 0, h, 0))
    return pl.pallas_call(
        functools.partial(inverse_kernel, chunks),
        grid=(halves, steps),
        in_specs=[pl.BlockSpec(memory_space=pltpu.SMEM)]
        + [moved] * (2 * chunks)
        + [pl.BlockSpec((row_count, lon), lambda h, t: (0, 0))],
        out_specs=pl.BlockSpec((step_levels, rows, lon), lambda h, t: (h * steps + t, 0, 0)),
        out_shape=jax.ShapeDtypeStruct((levels, rows, lon), jnp.bfloat16),
        scratch_shapes=[pltpu.VMEM((row_count * PACK, LANES), jnp.float32)],
        compiler_params=pltpu.CompilerParams(vmem_limit_bytes=VMEM),
        cost_estimate=pl.CostEstimate(
            flops=2 * levels * rows * lon * row_count,
            bytes_accessed=2 * (levels * rows * (lon + 2 * row_count) + table.size),
            transcendentals=0,
        ),
    )(sign.reshape(1), *own, *other, table)


def mode_maps(modes_in, modes_out, places, lines, parts):
    modes, levels = modes_in.shape
    groups = lines // 2
    same = jnp.eye(2, dtype=modes_in.dtype)
    inward = modes_in.reshape(modes, places, groups, parts)
    inward = jnp.einsum("kvqb,cd->ckbvdq", inward, same).reshape(2 * modes, 2 * levels)
    outward = modes_out.reshape(places, groups, parts, modes)
    outward = jnp.einsum("vqbk,cd->bvdqck", outward, same).reshape(2 * levels, 2 * modes)
    return inward, outward


def aligned_shards(grid_state, legendre, wave_order, lat_order, eig_rates, modes_in, modes_out):
    levels, _, rows, lon_count = grid_state.shape
    wave_count = wave_order.shape[0]
    half_rows = lat_order.shape[0]
    half_count = legendre.shape[3]
    slots = legendre.shape[0]
    waves = lax.axis_size("wave")
    places = lax.axis_size("level")
    parity = lax.axis_index("fld")
    wave_place = lax.axis_index("wave")
    level_place = lax.axis_index("level")
    owners = waves * places
    lat_rows = lax.dynamic_slice_in_dim(lat_order, wave_place * rows, rows)
    sine = jnp.sin((lat_rows.astype(jnp.float32) + 0.5) * (math.pi / (2.0 * half_rows)))
    hemi_sign = 1.0 - 2.0 * parity.astype(jnp.float32)
    coupling = (0.5 * hemi_sign * sine)[None, :, None]
    table = selected_table(wave_order, lon_count)
    own_waves = lax.dynamic_slice_in_dim(
        wave_order, (wave_place * places + level_place) * slots, slots
    )
    mask = triangle_mask(own_waves, parity, half_count, wave_count)[:, None, :]
    degree_f = degrees(own_waves, parity, half_count).astype(jnp.float32)
    ratio = tau_scale * degree_f * (degree_f + 1.0) / float(wave_count * (wave_count - 1))
    ratio = ratio[:, None, :]
    parts = LANES // rows
    groups = levels * rows // LANES
    lines = 2 * groups
    inward, outward = mode_maps(modes_in, modes_out, places, lines, parts)
    state = grid_state.reshape(levels, rows, lon_count)
    own_table = legendre.reshape(slots, half_rows, half_count)
    chunks = math.gcd(SLOT_CHUNKS, slots)
    chunk = slots // chunks
    by_owner = table.reshape(owners, chunks, 2 * chunk, lon_count)
    back_own, back_other = [], []
    for part in range(chunks):
        rows_here = forward_rows(state, by_owner[:, part].reshape(-1, lon_count), coupling)
        mirror = partner(rows_here, "fld", 0)
        mirrored = (
            mirror.astype(jnp.float32) + hemi_sign * rows_here.astype(jnp.float32)
        ).astype(jnp.bfloat16)
        mirrored = mirrored.reshape(owners, chunk, lines, LANES)
        data = lax.all_to_all(mirrored, ("wave", "level"), split_axis=0, concat_axis=0, tiled=True)
        coeffs = spectral_step(
            data.reshape(waves, places, chunk, lines, LANES),
            own_table,
            part * chunk,
            mask,
            ratio,
            eig_rates,
            inward,
            outward,
            rows,
        )
        back = lax.all_to_all(
            coeffs.reshape(owners, chunk, lines, LANES),
            ("wave", "level"),
            split_axis=0,
            concat_axis=0,
            tiled=True,
        ).reshape(owners, 2 * chunk, groups, LANES)
        back_own.append(back)
        back_other.append(partner(back, "fld", 0))
    out = inverse_rows(back_own, back_other, table, hemi_sign, levels, rows)
    return out.reshape(grid_state.shape)


def shards(grid_state, legendre, *rest):
    levels, _, rows, lon_count = grid_state.shape
    aligned = (
        rows % PACK == 0
        and LANES % rows == 0
        and (levels * rows) % (LANES * PACK) == 0
        and levels % (max(1, 256 // rows) * (levels * rows // (LANES * PACK))) == 0
        and lon_count % LANES == 0
    )
    run = aligned_shards if aligned else general_shards
    return run(grid_state, legendre, *rest)


def solution(mesh):
    placed = (
        P(("member", "level"), "fld", "wave", None),
        P(("wave", "level"), "fld", None, None),
        P(),
        P(),
        P(),
        P(),
        P(),
    )
    return jax.shard_map(
        shards,
        mesh=mesh,
        in_specs=placed,
        out_specs=P(("member", "level"), "fld", "wave", None),
        check_vma=False,
    )
```

```python
import functools
import math

import jax
import jax.numpy as jnp
import numpy as np
from jax import lax
from jax.experimental import pallas as pl
from jax.experimental.pallas import tpu as pltpu
from jax.sharding import PartitionSpec as P

LANES = 128
PACK = 16
SLOT_CHUNKS = 2
SLOTS_PER_STEP = 4
VMEM = 60 * 1024 * 1024

tau_scale = 2.0


def partner(value, axis, stride):
    mask = 2**stride
    pairs = [(source, source ^ mask) for source in range(lax.axis_size(axis))]
    return lax.ppermute(value, axis, pairs)


def fourier_table(wave_order, lon_count):
    longitude = jnp.arange(lon_count, dtype=jnp.int32)
    phase_index = longitude[:, None] * wave_order[None, :] % lon_count
    angles = phase_index.astype(jnp.float32) * (2.0 * math.pi / lon_count)
    weight_scale = math.sqrt(2.0 / lon_count)
    return jnp.concatenate(
        [jnp.cos(angles) * weight_scale, -jnp.sin(angles) * weight_scale], axis=1
    ).astype(jnp.bfloat16)


def degrees(wave_ids, parity, half_count):
    return wave_ids[:, None] + 2 * jnp.arange(half_count, dtype=jnp.int32)[None, :] + parity


def triangle_mask(wave_ids, parity, half_count, wave_count):
    return (degrees(wave_ids, parity, half_count) <= wave_count - 1).astype(jnp.float32)


def damping(wave_ids, parity, half_count, wave_count, eig_rates):
    degree_f = degrees(wave_ids, parity, half_count).astype(jnp.float32)
    damp_ratio = tau_scale * degree_f * (degree_f + 1.0) / float(wave_count * (wave_count - 1))
    return 1.0 / (1.0 + damp_ratio[:, :, None] * eig_rates[None, None, :])


def forward_legendre(mirrored, table_part, in_triangle):
    spectral = jnp.einsum(
        "lhrcs,shrj->sjcl", mirrored, table_part, preferred_element_type=jnp.float32
    )
    return (spectral * in_triangle[:, :, None, None]).astype(jnp.bfloat16)


def inverse_legendre(solved, table_part):
    return jnp.einsum(
        "sjcl,shrj->lhrcs", solved, table_part, preferred_element_type=jnp.float32
    ).astype(jnp.bfloat16)


def implicit_solve(columns, factor, modes_in, modes_out):
    modal = jnp.einsum("sjcl,kl->sjck", columns, modes_in, preferred_element_type=jnp.float32)
    modal = (modal * factor[:, :, None, :]).astype(jnp.bfloat16)
    return jnp.einsum("sjck,lk->sjcl", modal, modes_out, preferred_element_type=jnp.float32).astype(
        jnp.bfloat16
    )


def general_shards(grid_state, legendre, wave_order, lat_order, eig_rates, modes_in, modes_out):
    lon_count = grid_state.shape[3]
    rows_here = grid_state.shape[2]
    wave_count = wave_order.shape[0]
    half_rows = lat_order.shape[0]
    half_count = legendre.shape[3]
    wave_size = lax.axis_size("wave")
    level_size = lax.axis_size("level")
    parity = lax.axis_index("fld")
    wave_place = lax.axis_index("wave")
    level_place = lax.axis_index("level")
    wave_table = fourier_table(wave_order, lon_count)
    lat_rows = lax.dynamic_slice_in_dim(lat_order, wave_place * rows_here, rows_here)
    sine = jnp.sin((lat_rows.astype(jnp.float32) + 0.5) * (math.pi / (2.0 * half_rows)))
    hemi_sign = 1.0 - 2.0 * parity.astype(jnp.float32)
    coupling = (0.5 * hemi_sign * sine)[None, None, :, None]
    wide_count = wave_count // wave_size
    narrow_count = wide_count // level_size
    wide_start = wave_place * wide_count
    narrow_start = wide_start + level_place * narrow_count
    wide_waves = lax.dynamic_slice_in_dim(wave_order, wide_start, wide_count)
    narrow_waves = lax.dynamic_slice_in_dim(wave_order, narrow_start, narrow_count)
    factor = damping(narrow_waves, parity, half_count, wave_count, eig_rates)
    wide_table = lax.all_gather(legendre, "level", axis=0, tiled=True)
    wide_mask = triangle_mask(wide_waves, parity, half_count, wave_count)
    initial = grid_state.astype(jnp.float32)
    current = grid_state
    forcing = (initial + coupling * jnp.tanh(current.astype(jnp.float32))).astype(jnp.bfloat16)
    fourier_rows = jnp.einsum(
        "lhrg,gk->lhrk", forcing, wave_table, preferred_element_type=jnp.float32
    )
    fourier_rows = fourier_rows.astype(jnp.bfloat16).reshape(
        fourier_rows.shape[:3] + (2, wave_count)
    )
    mirror_part = partner(fourier_rows, "fld", 0)
    mirrored = (
        mirror_part.astype(jnp.float32) + hemi_sign * fourier_rows.astype(jnp.float32)
    ).astype(jnp.bfloat16)
    gathered = lax.all_to_all(mirrored, "wave", split_axis=4, concat_axis=2, tiled=True)
    spectral = forward_legendre(gathered, wide_table, wide_mask)
    columns = lax.all_to_all(spectral, "level", split_axis=0, concat_axis=3, tiled=True)
    solved = implicit_solve(columns, factor, modes_in, modes_out)
    level_rows = lax.all_to_all(solved, "level", split_axis=3, concat_axis=0, tiled=True)
    grid_coeffs = inverse_legendre(level_rows, wide_table)
    grid_coeffs = lax.all_to_all(grid_coeffs, "wave", split_axis=2, concat_axis=4, tiled=True)
    mirror_back = partner(grid_coeffs, "fld", 0)
    hemi_grid = (
        0.5 * (mirror_back.astype(jnp.float32) + hemi_sign * grid_coeffs.astype(jnp.float32))
    ).astype(jnp.bfloat16)
    flat_coeffs = hemi_grid.reshape(hemi_grid.shape[:3] + (2 * wave_count,))
    current = jnp.einsum(
        "lhrk,gk->lhrg", flat_coeffs, wave_table, preferred_element_type=jnp.float32
    ).astype(jnp.bfloat16)
    return current


def selected_table(wave_order, wave_count, lon_count):
    phase = np.arange(wave_count)[:, None] * np.arange(lon_count)[None, :] % lon_count
    angles = phase * (2.0 * math.pi / lon_count)
    rows = np.stack([np.cos(angles), -np.sin(angles)], axis=1) * math.sqrt(2.0 / lon_count)
    rows = jnp.asarray(rows.reshape(2 * wave_count, lon_count).astype(np.float32), jnp.bfloat16)
    wanted = 2 * wave_order[:, None] + jnp.arange(2, dtype=jnp.int32)[None, :]
    held = jnp.arange(2 * wave_count, dtype=jnp.int32)
    pick = (wanted.reshape(-1, 1) == held[None, :]).astype(jnp.bfloat16)
    return jnp.dot(pick, rows, preferred_element_type=jnp.float32).astype(jnp.bfloat16)


def forward_kernel(coupling_ref, state_ref, table_ref, out_ref, turned):
    step = pl.program_id(1)
    levels, rows, lon = state_ref.shape
    groups = levels * rows // LANES
    initial = state_ref[...].astype(jnp.float32)
    forcing = (initial + coupling_ref[...] * jnp.tanh(initial)).astype(jnp.bfloat16)
    forcing = forcing.reshape(levels * rows, lon)
    coeffs = lax.dot_general(
        table_ref[...], forcing, (((1,), (1,)), ((), ())), preferred_element_type=jnp.float32
    )
    for group in range(groups):
        turned[pl.ds(step * groups + group, coeffs.shape[0], stride=PACK), :] = coeffs[
            :, group * LANES : (group + 1) * LANES
        ]

    @pl.when(step == pl.num_programs(1) - 1)
    def _():
        out_ref[...] = turned[...].reshape(out_ref.shape).astype(jnp.bfloat16)


def forward_rows(state, table, coupling):
    levels, rows, lon = state.shape
    row_count = table.shape[0]
    halves = levels * rows // (LANES * PACK)
    step_levels = max(1, 512 // rows)
    steps = levels // halves // step_levels
    return pl.pallas_call(
        forward_kernel,
        grid=(halves, steps),
        in_specs=[
            pl.BlockSpec((1, rows, 1), lambda h, t: (0, 0, 0)),
            pl.BlockSpec((step_levels, rows, lon), lambda h, t: (h * steps + t, 0, 0)),
            pl.BlockSpec((row_count, lon), lambda h, t: (0, 0)),
        ],
        out_specs=pl.BlockSpec((row_count, PACK, LANES), lambda h, t: (0, h, 0)),
        out_shape=jax.ShapeDtypeStruct((row_count, halves * PACK, LANES), jnp.bfloat16),
        scratch_shapes=[pltpu.VMEM((row_count * PACK, LANES), jnp.float32)],
        compiler_params=pltpu.CompilerParams(vmem_limit_bytes=VMEM),
        cost_estimate=pl.CostEstimate(
            flops=2 * levels * rows * lon * row_count,
            bytes_accessed=2 * (state.size + table.size + row_count * levels * rows),
            transcendentals=state.size,
        ),
    )(coupling, state, table)


def spectral_kernel(rows, data_ref, table_ref, mask_ref, ratio_ref, eig_ref, in_ref, out_modes, out_ref):
    waves, places, slots, lines, _ = data_ref.shape
    parts = LANES // rows
    modes = eig_ref.shape[0]
    for slot in range(slots):
        picked = []
        for part in range(parts):
            for place in range(places):
                picked.append(
                    jnp.concatenate(
                        [
                            data_ref[wave, place, slot][:, part * rows : (part + 1) * rows]
                            for wave in range(waves)
                        ],
                        axis=1,
                    )
                )
        table = table_ref[slot]
        spectral = jnp.dot(
            jnp.concatenate(picked, axis=0), table, preferred_element_type=jnp.float32
        )
        spectral = (spectral * mask_ref[slot]).astype(jnp.bfloat16)
        modal = jnp.dot(in_ref[...], spectral, preferred_element_type=jnp.float32)
        factor = 1.0 / (1.0 + eig_ref[...] * ratio_ref[slot])
        modal = jnp.concatenate(
            [modal[:modes] * factor, modal[modes:] * factor], axis=0
        ).astype(jnp.bfloat16)
        solved = jnp.dot(out_modes[...], modal, preferred_element_type=jnp.float32)
        coeffs = lax.dot_general(
            solved.astype(jnp.bfloat16),
            table,
            (((1,), (1,)), ((), ())),
            preferred_element_type=jnp.float32,
        ).astype(jnp.bfloat16)
        for wave in range(waves):
            for place in range(places):
                out_ref[wave, place, slot] = jnp.concatenate(
                    [
                        coeffs[
                            (part * places + place) * lines : (part * places + place + 1) * lines,
                            wave * rows : (wave + 1) * rows,
                        ]
                        for part in range(parts)
                    ],
                    axis=1,
                )


def spectral_step(data, legendre, first, mask, ratio, eig_rates, inward, outward, rows):
    waves, places, slots, lines, _ = data.shape
    half_rows, half_count = legendre.shape[1:]
    modes = eig_rates.shape[0]
    block = math.gcd(slots, SLOTS_PER_STEP)
    skip = first // block
    whole = pl.BlockSpec(inward.shape, lambda i: (0, 0))
    vector = pl.BlockSpec((block, 1, half_count), lambda i: (i + skip, 0, 0))
    moved = pl.BlockSpec((waves, places, block, lines, LANES), lambda i: (0, 0, i, 0, 0))
    return pl.pallas_call(
        functools.partial(spectral_kernel, rows),
        grid=(slots // block,),
        in_specs=[
            moved,
            pl.BlockSpec((block, half_rows, half_count), lambda i: (i + skip, 0, 0)),
            vector,
            vector,
            pl.BlockSpec((modes, 1), lambda i: (0, 0)),
            whole,
            whole,
        ],
        out_specs=moved,
        out_shape=jax.ShapeDtypeStruct(data.shape, jnp.bfloat16),
        compiler_params=pltpu.CompilerParams(vmem_limit_bytes=VMEM),
        cost_estimate=pl.CostEstimate(
            flops=8 * slots * half_rows * half_count * inward.shape[0],
            bytes_accessed=2 * (2 * data.size + slots * half_rows * half_count),
            transcendentals=0,
        ),
    )(data, legendre, mask, ratio, eig_rates.reshape(-1, 1), inward, outward)


def inverse_kernel(sign_ref, own_ref, other_ref, table_ref, *refs):
    sum_refs, (out_ref, turned) = refs[:-2], refs[-2:]
    step = pl.program_id(1)
    levels, rows, lon = out_ref.shape
    groups = levels * rows // LANES
    row_count = own_ref.shape[0]

    @pl.when(step == 0)
    def _():
        own = own_ref[...].astype(jnp.float32)
        other = other_ref[...].astype(jnp.float32)
        grid = (0.5 * (other + sign_ref[0] * own)).astype(jnp.bfloat16)
        turned[...] = grid.astype(jnp.float32).reshape(-1, LANES)

    picked = jnp.concatenate(
        [
            turned[pl.ds(step * groups + group, row_count, stride=PACK), :].astype(jnp.bfloat16)
            for group in range(groups)
        ],
        axis=1,
    )
    out = lax.dot_general(
        picked, table_ref[...], (((0,), (0,)), ((), ())), preferred_element_type=jnp.float32
    ).reshape(out_ref.shape)
    for sum_ref in sum_refs:
        out = out + sum_ref[...]
    out_ref[...] = out.astype(out_ref.dtype)


def inverse_rows(own, other, table, sign, so_far, levels, rows, dtype):
    row_count, lon = table.shape
    halves = levels * rows // (LANES * PACK)
    step_levels = max(1, 512 // rows)
    steps = levels // halves // step_levels
    moved = pl.BlockSpec((row_count, PACK, LANES), lambda h, t: (0, h, 0))
    result = pl.BlockSpec((step_levels, rows, lon), lambda h, t: (h * steps + t, 0, 0))
    return pl.pallas_call(
        inverse_kernel,
        grid=(halves, steps),
        in_specs=[
            pl.BlockSpec(memory_space=pltpu.SMEM),
            moved,
            moved,
            pl.BlockSpec((row_count, lon), lambda h, t: (0, 0)),
        ]
        + [result] * len(so_far),
        out_specs=result,
        out_shape=jax.ShapeDtypeStruct((levels, rows, lon), dtype),
        scratch_shapes=[pltpu.VMEM((row_count * PACK, LANES), jnp.float32)],
        compiler_params=pltpu.CompilerParams(vmem_limit_bytes=VMEM),
        cost_estimate=pl.CostEstimate(
            flops=2 * levels * rows * lon * row_count,
            bytes_accessed=2 * (levels * rows * (3 * lon + 2 * row_count) + table.size),
            transcendentals=0,
        ),
    )(sign.reshape(1), own, other, table, *so_far)


def untouched(*refs):
    del refs


def after(value, done):
    anywhere = pl.BlockSpec(memory_space=pl.ANY)
    return pl.pallas_call(
        untouched,
        in_specs=[anywhere] * (1 + len(done)),
        out_specs=anywhere,
        out_shape=jax.ShapeDtypeStruct(value.shape, value.dtype),
        input_output_aliases={0: 0},
    )(value, *done)


def mode_maps(modes_in, modes_out, places, lines, parts):
    modes, levels = modes_in.shape
    groups = lines // 2
    same = jnp.eye(2, dtype=modes_in.dtype)
    inward = modes_in.reshape(modes, places, groups, parts)
    inward = jnp.einsum("kvqb,cd->ckbvdq", inward, same).reshape(2 * modes, 2 * levels)
    outward = modes_out.reshape(places, groups, parts, modes)
    outward = jnp.einsum("vqbk,cd->bvdqck", outward, same).reshape(2 * levels, 2 * modes)
    return inward, outward


def aligned_shards(grid_state, legendre, wave_order, lat_order, eig_rates, modes_in, modes_out):
    levels, _, rows, lon_count = grid_state.shape
    wave_count = wave_order.shape[0]
    half_rows = lat_order.shape[0]
    half_count = legendre.shape[3]
    slots = legendre.shape[0]
    waves = lax.axis_size("wave")
    places = lax.axis_size("level")
    parity = lax.axis_index("fld")
    wave_place = lax.axis_index("wave")
    level_place = lax.axis_index("level")
    owners = waves * places
    lat_rows = lax.dynamic_slice_in_dim(lat_order, wave_place * rows, rows)
    sine = jnp.sin((lat_rows.astype(jnp.float32) + 0.5) * (math.pi / (2.0 * half_rows)))
    hemi_sign = 1.0 - 2.0 * parity.astype(jnp.float32)
    coupling = (0.5 * hemi_sign * sine)[None, :, None]
    own_waves = lax.dynamic_slice_in_dim(
        wave_order, (wave_place * places + level_place) * slots, slots
    )
    mask = triangle_mask(own_waves, parity, half_count, wave_count)[:, None, :]
    degree_f = degrees(own_waves, parity, half_count).astype(jnp.float32)
    ratio = tau_scale * degree_f * (degree_f + 1.0) / float(wave_count * (wave_count - 1))
    ratio = ratio[:, None, :]
    parts = LANES // rows
    groups = levels * rows // LANES
    lines = 2 * groups
    inward, outward = mode_maps(modes_in, modes_out, places, lines, parts)
    state = grid_state.reshape(levels, rows, lon_count)
    own_table = legendre.reshape(slots, half_rows, half_count)
    chunks = math.gcd(SLOT_CHUNKS, slots)
    chunk = slots // chunks
    by_owner = wave_order.reshape(owners, chunks, chunk)
    tables, backs = [], []
    for part in range(chunks):
        table = selected_table(by_owner[:, part].reshape(-1), wave_count, lon_count)
        rows_here = forward_rows(state, table, coupling)
        mirror = partner(rows_here, "fld", 0)
        mirrored = (
            mirror.astype(jnp.float32) + hemi_sign * rows_here.astype(jnp.float32)
        ).astype(jnp.bfloat16)
        mirrored = mirrored.reshape(owners, chunk, lines, LANES)
        data = lax.all_to_all(mirrored, ("wave", "level"), split_axis=0, concat_axis=0, tiled=True)
        coeffs = spectral_step(
            data.reshape(waves, places, chunk, lines, LANES),
            own_table,
            part * chunk,
            mask,
            ratio,
            eig_rates,
            inward,
            outward,
            rows,
        )
        back = lax.all_to_all(
            coeffs.reshape(owners, chunk, lines, LANES),
            ("wave", "level"),
            split_axis=0,
            concat_axis=0,
            tiled=True,
        ).reshape(owners * 2 * chunk, groups, LANES)
        tables.append(table)
        backs.append(back)
    so_far = []
    for part in range(chunks):
        dtype = jnp.bfloat16 if part == chunks - 1 else jnp.bfloat16
        own = after(backs[part], so_far) if so_far else backs[part]
        other = partner(own, "fld", 0)
        out = inverse_rows(own, other, tables[part], hemi_sign, so_far, levels, rows, dtype)
        so_far = [out]
    return out.reshape(grid_state.shape)


def shards(grid_state, legendre, *rest):
    levels, _, rows, lon_count = grid_state.shape
    aligned = (
        rows % PACK == 0
        and LANES % rows == 0
        and (levels * rows) % (LANES * PACK) == 0
        and levels % (max(1, 512 // rows) * (levels * rows // (LANES * PACK))) == 0
        and lon_count % LANES == 0
    )
    run = aligned_shards if aligned else general_shards
    return run(grid_state, legendre, *rest)


def solution(mesh):
    placed = (
        P(("member", "level"), "fld", "wave", None),
        P(("wave", "level"), "fld", None, None),
        P(),
        P(),
        P(),
        P(),
        P(),
    )
    return jax.shard_map(
        shards,
        mesh=mesh,
        in_specs=placed,
        out_specs=P(("member", "level"), "fld", "wave", None),
        check_vma=False,
    )
```
